32 devices in a mesh: grp: 2 (over y), inter: 4 (over z), intra: 4 (over x, core).
Axes of the slice: x: 2, y: 2, z: 4, core: 2. Of those that a mesh axis runs over, the one named last changes fastest.
Arguments:
- hidden: bfloat16 [4, 768, 8192], P('grp', 'inter', 'intra'), parts along dimension 0, may hold values from -20 to 20
- w_query: bfloat16 [8192, 4096], P('inter', 'intra'), may hold values from -2 to 2
- w_keyval: bfloat16 [8192, 1024], P('inter', 'intra'), may hold values from -1 to 1
- b_query: bfloat16 [4096], P('intra'), may hold values from -3 to 3
- b_keyval: bfloat16 [1024], P('intra'), may hold values from -3 to 3
- segments: int32 [4, 4, 192], P('grp', 'inter'), parts along dimension 0, may hold values from 0 to 8, never falling along the last dimension, each value on 1 to 48 neighbouring positions
Outputs:
- context: bfloat16 [4, 768, 4096], P('grp', 'inter', 'intra'), parts along dimension 0
The draws below stay inside these ranges and needn't reach their ends.
There are 2 independent parts, one for each index of `grp`. The reference program is written for one: setup_inputs(seed, part) draws one part's arguments, and reference() takes and returns one part's arrays. A program takes and returns all parts, laid end to end along the dimension named above; an argument that names none is the same for every part. Nothing has to cross between parts.
Inputs may be any that keep to these rules, and one draw needn't show every extreme that they name: `segments`: in every block the segment numbers never fall, every number of 0 to 8 occurs, and each segment has 1 to 48 tokens.
All inputs are finite; a program needn't handle non-finite values.
Results may differ from the reference program's by a relative error of at most 0.0075.
Values may be sent and summed in bfloat16 or wider, within the bound.
A program may use at most 128 MiB of HBM per device.

```python
import math
import jax
import jax.numpy as jnp
import numpy as np
from jax import lax

D = 8192
QH = 32
KV = 4
HD = 128
RESP = 8
MICRO = 2
TOK = 192
N_INTER = 4


def key_rows(key):
    return jnp.clip(jax.random.normal(key, (D, KV, HD), jnp.float32), -6.0, 6.0)


def draw_hidden(key, part):
    key = jax.random.fold_in(key, 11)
    keys = jax.random.split(key, 2)
    scale = jnp.exp(jax.random.uniform(keys[0], (D,), jnp.float32, -0.7, 0.7))
    result = jnp.clip(jax.random.normal(keys[1], (MICRO, N_INTER * TOK, D), jnp.float32), -6.0, 6.0) * scale
    return result.astype(jnp.bfloat16)


def draw_w_query(key, part):
    key = jax.random.fold_in(key, 12)
    own = jnp.clip(jax.random.normal(key, (D, QH * HD), jnp.float32), -6.0, 6.0)
    result = own
    return (result * D ** (-0.5)).astype(jnp.bfloat16)


def draw_w_keyval(key, part):
    common = key_rows(key)
    key = jax.random.fold_in(key, 13)
    values = jnp.clip(jax.random.normal(key, (D, KV, HD), jnp.float32), -6.0, 6.0)
    result = jnp.stack([common, values], axis=1).reshape(D, 2 * KV * HD)
    return (result * D ** (-0.5)).astype(jnp.bfloat16)


def levels(own_key, shape, shards, low, largest):
    level = 1.0
    for axis_at, blocks in shards:
        draws = jax.random.uniform(jax.random.fold_in(jax.random.fold_in(own_key, 6), axis_at), (blocks,), jnp.float32, low / len(shards), largest / len(shards))
        level = level * jnp.repeat(jnp.exp(draws), shape[axis_at] // blocks).reshape((-1,) + (1,) * (len(shape) - 1 - axis_at))
    return level


def profile(amount, total, bound, lean):
    weights = [(1 << 20) // math.isqrt(grade ** lean) + 1 for grade in range(2, amount + 1)]
    rest, given = total - bound - (amount - 1), [1] * (amount - 1)
    while rest > 0:
        movable = [i for i in range(amount - 1) if given[i] < bound]
        mass, budget = sum([weights[i] for i in movable]), rest
        for i in movable:
            extra = min(bound - given[i], max(1, budget * weights[i] // mass), rest)
            given[i] = given[i] + extra
            rest = rest - extra
    return np.array([bound] + given)


def uneven_parts(own_key, amount, total, bound, lean):
    if amount == 2:
        one = jax.random.randint(own_key, (), max(1, total - bound), min(bound, total - 1) + 1)
        return jnp.stack([one, total - one])
    lengths = jnp.asarray(profile(amount, total, bound, lean), jnp.int32)
    pairs = (amount - 1) // 2
    source_of, sink = lengths[1:1 + 2 * pairs:2], lengths[2:2 + 2 * pairs:2]
    room = jnp.minimum(source_of - 1, bound - sink)
    shifted = jax.random.randint(jax.random.fold_in(own_key, 1), (pairs,), 0, 1 << 20) % (room + 1)
    lengths = lengths.at[1:1 + 2 * pairs:2].set(source_of - shifted).at[2:2 + 2 * pairs:2].set(sink + shifted)
    return lengths[jax.random.permutation(jax.random.fold_in(own_key, 2), amount)]


def bell_draw(stream_key, dims, scale, most, cuts=(), kind=jnp.bfloat16):
    values = jax.random.normal(stream_key, dims, jnp.float32) * scale
    if len(cuts) > 0:
        values = levels(stream_key, dims, cuts, -0.22, 0.18) * values
    return jnp.clip(values, min=-most, max=most).astype(kind)


def setup_inputs(seed: int = 0, part: int = 0) -> dict:
    streams_of = jax.random.split(jax.random.key(seed), 7)
    part_keys = jax.random.split(jax.random.fold_in(streams_of[6], part), 7)
    return {
        "hidden": draw_hidden(jax.random.fold_in(jax.random.fold_in(streams_of[6], part), 71), part),
        "w_query": draw_w_query(jax.random.fold_in(streams_of[6], 71), part),
        "w_keyval": draw_w_keyval(jax.random.fold_in(streams_of[6], 71), part),
        "b_query": bell_draw(streams_of[3], (QH * HD,), 0.5, 3.0, ((0, 4),)),
        "b_keyval": bell_draw(streams_of[4], (2 * KV * HD,), 0.5, 3.0, ((0, 4),)),
        "segments": jax.vmap(lambda own: jnp.searchsorted(jnp.cumsum(uneven_parts(own, RESP + 1, TOK, TOK // 4, 0)), jnp.arange(TOK), side="right"))(jax.random.split(part_keys[5], MICRO * N_INTER)).reshape((MICRO, N_INTER, TOK)).astype(jnp.int32),
    }


def positions(segments):
    prefix = jnp.sum((segments == 0).astype(jnp.int32), axis=-1, keepdims=True).astype(jnp.int32)
    below = jnp.sum((segments[..., None, :] < segments[..., :, None]).astype(jnp.int32), axis=-1).astype(jnp.int32)
    places = lax.broadcasted_iota(jnp.int32, segments.shape, segments.ndim - 1)
    return (places - below + jnp.where(segments > 0, prefix, 0)).astype(jnp.int32)


def rotate(values, angles_pos):
    width = values.shape[-1]
    half = width // 2
    freq = 1000000.0 ** (-2.0 * jnp.arange(half, dtype=jnp.float32) / width)
    angles = angles_pos[..., None] * freq
    cosine = jnp.cos(angles)
    sine = jnp.sin(angles)
    first = values[..., :half]
    second = values[..., half:]
    return jnp.concatenate([first * cosine - second * sine, second * cosine + first * sine], axis=-1)


def reference(hidden, w_query, w_keyval, b_query, b_keyval, segments):
    batches, tokens, width = hidden.shape
    blocks = segments.shape[1]
    block_len = segments.shape[2]
    flat = hidden.reshape(batches * tokens, width)
    query = jnp.dot(flat, w_query, preferred_element_type=jnp.float32) + b_query.astype(jnp.float32)
    keyval = jnp.dot(flat, w_keyval, preferred_element_type=jnp.float32) + b_keyval.astype(jnp.float32)
    place_pos = positions(segments).reshape(batches * tokens).astype(jnp.float32)
    query = rotate(query.reshape(batches * tokens, QH, HD), place_pos[:, None]).astype(jnp.bfloat16)
    keyval = keyval.reshape(batches * tokens, 2, KV, HD)
    keys = rotate(keyval[:, 0, :, :], place_pos[:, None]).astype(jnp.bfloat16)
    values = keyval[:, 1, :, :].astype(jnp.bfloat16)
    group = QH // KV
    query = query.reshape(batches, blocks, block_len, KV, group, HD).astype(jnp.float32)
    keys = keys.reshape(batches, blocks, block_len, KV, HD).astype(jnp.float32)
    values = values.reshape(batches, blocks, block_len, KV, HD).astype(jnp.float32)
    scores = jnp.einsum("bctkgd,bcskd->bckgts", query, keys) * (HD ** -0.5)
    later = jnp.arange(block_len, dtype=jnp.int32)
    causal = later[None, :] <= later[:, None]
    same = (segments[:, :, None, :] == 0) | (segments[:, :, None, :] == segments[:, :, :, None])
    allowed = (causal[None, None] & same)[:, :, None, None, :, :]
    scores = jnp.where(allowed, scores, -1e30)
    peak = jnp.max(scores, axis=-1, keepdims=True)
    expo = jnp.where(allowed, jnp.exp(scores - peak), 0.0)
    weights = (expo / jnp.sum(expo, axis=-1, keepdims=True)).astype(jnp.bfloat16)
    context = jnp.einsum("bckgts,bcskd->bctkgd", weights.astype(jnp.float32), values)
    return context.reshape(batches, tokens, QH * HD).astype(jnp.bfloat16)
```

```python
import functools

import jax
import jax.numpy as jnp
import numpy as np
from jax import lax
from jax.experimental import pallas as pl
from jax.experimental.pallas import tpu as pltpu
from jax.sharding import PartitionSpec as P

QH = 32
KV = 4
HD = 128
CORES = 2
MESH = pl.DeviceIdType.MESH


def kernel(n_inter, n_intra, hid, wq, wkv, bq, bkv, seg, freq, out,
           xg, wbuf, rb, cosb, sinb, maskb, kvs, kvb,
           wsem, hsend, hrecv, fsend, xsend, frecv, csend, crecv, kvsend, kvrecv):
    batches, block = seg.shape
    rows = batches * block
    depth = wkv.shape[0]
    width = wkv.shape[1]
    chunks = wbuf.shape[0]
    piece = rows // n_intra
    layers_each = n_inter // n_intra
    chips = n_intra // CORES
    i = lax.axis_index("inter")
    j = lax.axis_index("intra")
    xc = j // CORES
    core = lax.rem(j, CORES)
    sibling = xc * CORES + (CORES - 1 - core)
    total = n_inter * n_intra
    me = i * n_intra + j

    wcopies = [pltpu.make_async_copy(wkv, wbuf.at[0], wsem.at[0])]
    for c in range(chunks - 1):
        wcopies.append(pltpu.make_async_copy(
            wq.at[:, pl.ds(c * width, width)], wbuf.at[c + 1], wsem.at[c + 1]))
    for cp in wcopies:
        cp.start()

    barrier = pltpu.get_barrier_semaphore()

    @pl.loop(1, total)
    def _(k):
        other = lax.rem(me + k, total)
        pl.semaphore_signal(
            barrier, inc=1,
            device_id={"inter": other // n_intra, "intra": lax.rem(other, n_intra)},
            device_id_type=MESH)

    pl.semaphore_wait(barrier, total - 1)

    def remote(src, dst, ssem, rsem, ii, jj):
        return pltpu.make_async_remote_copy(
            src_ref=src, dst_ref=dst, send_sem=ssem, recv_sem=rsem,
            device_id={"inter": ii, "intra": jj}, device_id_type=MESH)

    def spread(gg, p):
        src = hid.at[pl.ds(p * piece, piece), pl.ds(gg * depth, depth)]
        dst = xg.at[i, pl.ds(p * piece, piece), :]
        return src, dst

    for gg in range(layers_each):
        layer = j * layers_each + gg
        for p in range(n_intra):
            src, dst = spread(gg, p)
            here = (layer == i) & (p == j)

            @pl.when(here)
            def _():
                pltpu.make_async_copy(src, dst, hrecv.at[i]).start()

            @pl.when(jnp.logical_not(here))
            def _():
                remote(src, dst, hsend.at[gg * n_intra + p], hrecv.at[i], layer, p).start()

    def part(t, p):
        return xg.at[t, pl.ds(pl.multiple_of(p * piece, piece), piece), :]

    fr = freq[...]
    lane = lax.broadcasted_iota(jnp.int32, (1, HD), 1)
    r_i = lax.broadcasted_iota(jnp.int32, (block, block), 0)
    c_i = lax.broadcasted_iota(jnp.int32, (block, block), 1)
    place = lax.broadcasted_iota(jnp.int32, (block, 1), 0).astype(jnp.float32)

    def tables():
        for b in range(batches):
            segr = seg[b:b + 1, :].astype(jnp.float32)
            segm = jnp.broadcast_to(segr, (block, block))
            segc = jnp.sum(jnp.where(r_i == c_i, segm, 0.0), axis=1, keepdims=True)
            below = jnp.sum(jnp.where(segm < segc, 1.0, 0.0), axis=1, keepdims=True)
            plen = jnp.sum(jnp.where(segm == 0.0, 1.0, 0.0), axis=1, keepdims=True)
            pos = place - below + jnp.where(segc > 0.0, plen, 0.0)
            angles = pos * fr
            cosb[b * block:(b + 1) * block, :] = jnp.cos(angles)
            sine = jnp.sin(angles)
            sinb[b * block:(b + 1) * block, :] = jnp.where(lane < HD // 2, -sine, sine)
            allowed = (c_i <= r_i) & ((segm == 0.0) | (segm == segc))
            maskb[b] = jnp.where(allowed, 0.0, -1e30)

    def own_copies(t):
        res = []
        for k in range(1, chips):
            ox = lax.rem(xc + k, chips)
            res.append(remote(part(t, j), part(t, j), fsend.at[t, k], frecv.at[t, j],
                              i, ox * CORES + core))
        res.append(remote(part(t, j), part(t, j), fsend.at[t, 0], frecv.at[t, j], i, sibling))
        return res

    def cross_copies(t):
        res = []
        for k in range(1, chips):
            p = lax.rem(xc + k, chips) * CORES + core
            res.append(remote(part(t, p), part(t, p), xsend.at[t, k - 1], frecv.at[t, p],
                              i, sibling))
        return res

    def arrived(t, p):
        pltpu.make_async_copy(part(t, p), part(t, p), frecv.at[t, p]).wait()

    def order(k):
        return lax.rem(i + k, n_inter)

    @pl.loop(0, n_inter + 1)
    def _(k):
        @pl.when(k < n_inter)
        def _():
            t = order(k)
            pltpu.make_async_copy(part(t, j), part(t, j), hrecv.at[t]).wait()
            for cp in own_copies(t):
                cp.start()

        @pl.when(k == 0)
        def _():
            tables()

        @pl.when(k > 0)
        def _():
            t = order(k - 1 + n_inter)
            for q in range(1, chips):
                arrived(t, lax.rem(xc + q, chips) * CORES + core)
            for cp in cross_copies(t):
                cp.start()

    for cp in wcopies:
        cp.wait()

    def ready(t):
        for q in range(chips):
            arrived(t, q * CORES + (CORES - 1 - core))

    def product(t, c):
        return jnp.dot(xg[t], wbuf[c], preferred_element_type=jnp.float32)

    def chain(t, c, slot, to):
        return remote(rb.at[t, c], rb.at[slot, c], csend.at[t, c], crecv.at[slot, c], to, j)

    def landed(slot, c):
        pltpu.make_async_copy(rb.at[slot, c], rb.at[slot, c], crecv.at[slot, c]).wait()

    def hop(t, c, has_before, slot, to):
        acc = product(t, c)

        @pl.when(has_before)
        def _():
            landed(t, c)
            rb[t, c] = (rb[t, c].astype(jnp.float32) + acc).astype(jnp.bfloat16)

        @pl.when(jnp.logical_not(has_before))
        def _():
            rb[t, c] = acc.astype(jnp.bfloat16)

        chain(t, c, slot, to).start()

    def down_slot(t):
        return jnp.where(t == i - 1, n_inter, t)

    @pl.loop(0, n_inter - 1)
    def _(s):
        up = n_inter - 1 - s
        down = s

        @pl.when(up > i)
        def _():
            ready(up)

        @pl.when(down < i)
        def _():
            ready(down)

        @pl.loop(0, chunks)
        def _(c):
            @pl.when(up > i)
            def _():
                hop(up, c, i > 0, up, i + 1)

            @pl.when(down < i)
            def _():
                hop(down, c, i < n_inter - 1, down_slot(down), i - 1)

    ready(i)

    def total_of(c):
        acc = product(i, c)
        zero = jnp.zeros_like(acc)

        @pl.when(i > 0)
        def _():
            landed(i, c)

        @pl.when(i < n_inter - 1)
        def _():
            landed(n_inter, c)

        acc = acc + jnp.where(i > 0, rb[i, c].astype(jnp.float32), zero)
        return acc + jnp.where(i < n_inter - 1, rb[n_inter, c].astype(jnp.float32), zero)

    def rot(u):
        return u * cosb[...] + pltpu.roll(u, HD // 2, 1) * sinb[...]

    @pl.when(i == 0)
    def _():
        rb[0] = jnp.zeros(rb.shape[1:], rb.dtype)

    @pl.when(i == n_inter - 1)
    def _():
        rb[n_inter] = jnp.zeros(rb.shape[1:], rb.dtype)

    here_kv = width // HD
    per = n_intra // KV
    acc = total_of(0) + bkv[...].astype(jnp.float32)
    for b in range(here_kv):
        gb = j * here_kv + b
        u = acc[:, b * HD:(b + 1) * HD]
        kvs[b] = jnp.where(gb < KV, rot(u), u).astype(jnp.bfloat16)

    def kv_copies(b, r):
        gb = j * here_kv + b
        dest = lax.rem(gb, KV) * per + r
        kind = gb // KV
        return dest, kind, remote(kvs.at[b], kvb.at[kind], kvsend.at[b * per + r],
                                  kvrecv.at[kind], i, dest)

    for b in range(here_kv):
        for r in range(per):
            dest, kind, cp = kv_copies(b, r)

            @pl.when(dest == j)
            def _():
                pltpu.make_async_copy(kvs.at[b], kvb.at[kind], kvrecv.at[kind]).start()

            @pl.when(dest != j)
            def _():
                cp.start()

    for kind in range(2):
        pltpu.make_async_copy(kvb.at[kind], kvb.at[kind], kvrecv.at[kind]).wait()

    for c in range(1, chunks):
        base = (c - 1) * width
        acc = total_of(c) + bq[:, base:base + width].astype(jnp.float32)
        for h in range(width // HD):
            qh = rot(acc[:, h * HD:(h + 1) * HD]).astype(jnp.bfloat16)
            for b in range(batches):
                lo = b * block
                sc = lax.dot_general(qh[lo:lo + block, :], kvb[0, lo:lo + block, :],
                                     (((1,), (1,)), ((), ())),
                                     preferred_element_type=jnp.float32)
                sc = sc * HD ** (-0.5) + maskb[b]
                peak = jnp.max(sc, axis=-1, keepdims=True)
                expo = jnp.exp(sc - peak)
                wts = (expo / jnp.sum(expo, axis=-1, keepdims=True)).astype(jnp.bfloat16)
                ctx = jnp.dot(wts, kvb[1, lo:lo + block, :], preferred_element_type=jnp.float32)
                out[lo:lo + block, base + h * HD:base + (h + 1) * HD] = ctx.astype(jnp.bfloat16)

    for gg in range(layers_each):
        layer = j * layers_each + gg
        for p in range(n_intra):
            src, dst = spread(gg, p)

            @pl.when(jnp.logical_not((layer == i) & (p == j)))
            def _():
                remote(src, dst, hsend.at[gg * n_intra + p], hrecv.at[i], layer, p).wait_send()

    @pl.loop(0, n_inter)
    def _(t):
        for cp in own_copies(t) + cross_copies(t):
            cp.wait_send()

        @pl.when(t != i)
        def _():
            @pl.loop(0, chunks)
            def _(c):
                chain(t, c, t, i).wait_send()

    for b in range(here_kv):
        for r in range(per):
            dest, kind, cp = kv_copies(b, r)

            @pl.when(dest != j)
            def _():
                cp.wait_send()


def local(n_inter, n_intra, hidden, w_query, w_keyval, b_query, b_keyval, segments):
    batches, block, feats = hidden.shape
    rows = batches * block
    depth, cols = w_query.shape
    width = w_keyval.shape[1]
    chunks = 1 + cols // width
    chips = n_intra // CORES
    half = HD // 2
    fr = 1000000.0 ** (-2.0 * np.arange(half, dtype=np.float64) / HD)
    freq = jnp.asarray(np.concatenate([fr, fr])[None, :], jnp.float32)
    vmem = pl.BlockSpec(memory_space=pltpu.VMEM)
    hbm = pl.BlockSpec(memory_space=pl.ANY)
    dma = pltpu.SemaphoreType.DMA
    here_kv = width // HD
    per = n_intra // KV
    result = pl.pallas_call(
        functools.partial(kernel, n_inter, n_intra),
        out_shape=jax.ShapeDtypeStruct((rows, cols), jnp.bfloat16),
        in_specs=[hbm, hbm, hbm, vmem, vmem, vmem, vmem],
        out_specs=vmem,
        scratch_shapes=[
            pltpu.VMEM((n_inter, rows, depth), jnp.bfloat16),
            pltpu.VMEM((chunks, depth, width), jnp.bfloat16),
            pltpu.VMEM((n_inter + 1, chunks, rows, width), jnp.bfloat16),
            pltpu.VMEM((rows, HD), jnp.float32),
            pltpu.VMEM((rows, HD), jnp.float32),
            pltpu.VMEM((batches, block, block), jnp.float32),
            pltpu.VMEM((here_kv, rows, HD), jnp.bfloat16),
            pltpu.VMEM((2, rows, HD), jnp.bfloat16),
            dma((chunks,)),
            dma((n_intra * (n_inter // n_intra),)),
            dma((n_inter,)),
            dma((n_inter, chips)),
            dma((n_inter, max(chips - 1, 1))),
            dma((n_inter, n_intra)),
            dma((n_inter, chunks)),
            dma((n_inter + 1, chunks)),
            dma((here_kv * per,)),
            dma((2,)),
        ],
        compiler_params=pltpu.CompilerParams(
            collective_id=0, has_side_effects=True, vmem_limit_bytes=52 * 2**20),
        name="project_attend",
    )(hidden.reshape(rows, feats), w_query, w_keyval, b_query[None, :], b_keyval[None, :],
      segments.reshape(batches, block), freq)
    return result.reshape(batches, block, cols)


def solution(mesh):
    in_specs = (
        P("grp", "inter", "intra"),
        P("inter", "intra"),
        P("inter", "intra"),
        P("intra"),
        P("intra"),
        P("grp", "inter", None),
    )
    out_specs = P("grp", "inter", "intra")
    body = functools.partial(local, mesh.shape["inter"], mesh.shape["intra"])
    return jax.shard_map(body, mesh=mesh, in_specs=in_specs, out_specs=out_specs, check_vma=False)
```

```python
import functools
import math

import jax
import jax.numpy as jnp
from jax import lax
from jax.experimental import pallas as pl
from jax.experimental.pallas import tpu as pltpu
from jax.sharding import PartitionSpec as P

QH = 32
KV = 4
HD = 128
CORES = 2
FALL = -2.0 * math.log(1000000.0) / HD
MESH = pl.DeviceIdType.MESH


def kernel(n_inter, n_intra, hid, wq, wkv, bq, bkv, seg, out,
           xg, stage, wbuf, rb, cosb, sinb, maskb, kvs, kvb,
           wsem, hsend, srecv, zsend, hrecv, fsend, xsend, frecv, csend, crecv, kvsend, kvrecv):
    batches, _, block = seg.shape
    rows = batches * block
    depth = wkv.shape[0]
    width = wkv.shape[1]
    chunks = wbuf.shape[0]
    piece = rows // n_intra
    layers_each = n_inter // n_intra
    chips = n_intra // CORES
    i = lax.axis_index("inter")
    j = lax.axis_index("intra")
    xc = j // CORES
    core = lax.rem(j, CORES)
    sibling = xc * CORES + (CORES - 1 - core)
    total = n_inter * n_intra
    me = i * n_intra + j

    wcopies = [pltpu.make_async_copy(wkv, wbuf.at[0], wsem.at[0])]
    for c in range(chunks - 1):
        wcopies.append(pltpu.make_async_copy(
            wq.at[:, pl.ds(c * width, width)], wbuf.at[c + 1], wsem.at[c + 1]))
    for cp in wcopies:
        cp.start()

    barrier = pltpu.get_barrier_semaphore()

    @pl.loop(1, total)
    def _(k):
        other = lax.rem(me + k, total)
        pl.semaphore_signal(
            barrier, inc=1,
            device_id={"inter": other // n_intra, "intra": lax.rem(other, n_intra)},
            device_id_type=MESH)

    pl.semaphore_wait(barrier, total - 1)

    def remote(src, dst, ssem, rsem, ii, jj):
        return pltpu.make_async_remote_copy(
            src_ref=src, dst_ref=dst, send_sem=ssem, recv_sem=rsem,
            device_id={"inter": ii, "intra": jj}, device_id_type=MESH)

    def spread(gg, p):
        layer = j * layers_each + gg
        src = hid.at[pl.ds(p * piece, piece), pl.ds(gg * depth, depth)]
        final = xg.at[i, pl.ds(p * piece, piece), :]
        sem = hsend.at[gg * n_intra + p]
        direct = remote(src, final, sem, hrecv.at[i], layer, p)
        detour = remote(src, stage.at[layer], sem, srecv.at[layer], i, p)
        keep = pltpu.make_async_copy(src, final, hrecv.at[i])
        here = (layer == i) & (p == j)
        straight = jnp.logical_not(here) & ((layer == i) | (p // CORES == xc))
        return here, straight, keep, direct, detour

    for gg in range(layers_each):
        for p in range(n_intra):
            here, straight, keep, direct, detour = spread(gg, p)

            @pl.when(here)
            def _():
                keep.start()

            @pl.when(straight)
            def _():
                direct.start()

            @pl.when(jnp.logical_not(here | straight))
            def _():
                detour.start()

    def part(t, p):
        return xg.at[t, pl.ds(pl.multiple_of(p * piece, piece), piece), :]

    def along(t):
        return remote(stage.at[t], part(i, j), zsend.at[t], hrecv.at[i], t, j)

    def detoured(t):
        return (t // layers_each) // CORES != xc

    def each(s, fn):
        up = n_inter - 1 - s

        @pl.when((s >= 0) & (up > i))
        def _():
            fn(up)

        @pl.when((s >= 0) & (s < i))
        def _():
            fn(s)

    def onward(t):
        @pl.when(detoured(t))
        def _():
            pltpu.make_async_copy(stage.at[t], stage.at[t], srecv.at[t]).wait()
            along(t).start()

    @pl.loop(0, n_inter - 1)
    def _(s):
        each(s, onward)

    lane = lax.broadcasted_iota(jnp.int32, (1, HD), 1)
    fr = jnp.exp(lax.rem(lane, HD // 2).astype(jnp.float32) * FALL)
    r_i = lax.broadcasted_iota(jnp.int32, (block, block), 0)
    c_i = lax.broadcasted_iota(jnp.int32, (block, block), 1)
    place = lax.broadcasted_iota(jnp.int32, (block, 1), 0).astype(jnp.float32)

    def tables():
        for b in range(batches):
            segr = seg[b].astype(jnp.float32)
            segm = jnp.broadcast_to(segr, (block, block))
            segc = jnp.sum(jnp.where(r_i == c_i, segm, 0.0), axis=1, keepdims=True)
            below = jnp.sum(jnp.where(segm < segc, 1.0, 0.0), axis=1, keepdims=True)
            plen = jnp.sum(jnp.where(segm == 0.0, 1.0, 0.0), axis=1, keepdims=True)
            pos = place - below + jnp.where(segc > 0.0, plen, 0.0)
            angles = pos * fr
            cosb[b * block:(b + 1) * block, :] = jnp.cos(angles)
            sine = jnp.sin(angles)
            sinb[b * block:(b + 1) * block, :] = jnp.where(lane < HD // 2, -sine, sine)
            allowed = (c_i <= r_i) & ((segm == 0.0) | (segm == segc))
            maskb[b] = jnp.where(allowed, 0.0, -1e30)

    def own_copies(t):
        res = []
        for k in range(1, chips):
            ox = lax.rem(xc + k, chips)
            res.append(remote(part(t, j), part(t, j), fsend.at[t, k], frecv.at[t, j],
                              i, ox * CORES + core))
        res.append(remote(part(t, j), part(t, j), fsend.at[t, 0], frecv.at[t, j], i, sibling))
        return res

    def cross_copies(t):
        res = []
        for k in range(1, chips):
            p = lax.rem(xc + k, chips) * CORES + core
            res.append(remote(part(t, p), part(t, p), xsend.at[t, k - 1], frecv.at[t, p],
                              i, sibling))
        return res

    def arrived(t, p):
        pltpu.make_async_copy(part(t, p), part(t, p), frecv.at[t, p]).wait()

    def own(t):
        pltpu.make_async_copy(part(t, j), part(t, j), hrecv.at[t]).wait()
        for cp in own_copies(t):
            cp.start()

    def cross(t):
        for q in range(1, chips):
            arrived(t, lax.rem(xc + q, chips) * CORES + core)
        for cp in cross_copies(t):
            cp.start()

    tables()

    for cp in wcopies:
        cp.wait()

    def ready(t):
        for q in range(chips):
            arrived(t, q * CORES + (CORES - 1 - core))

    def product(t, c):
        return jnp.dot(xg[t], wbuf[c], preferred_element_type=jnp.float32)

    def chain(t, c, slot, to):
        return remote(rb.at[t, c], rb.at[slot, c], csend.at[t, c], crecv.at[slot, c], to, j)

    def landed(slot, c):
        pltpu.make_async_copy(rb.at[slot, c], rb.at[slot, c], crecv.at[slot, c]).wait()

    def hop(t, c, has_before, slot, to):
        acc = product(t, c)

        @pl.when(has_before)
        def _():
            landed(t, c)
            rb[t, c] = (rb[t, c].astype(jnp.float32) + acc).astype(jnp.bfloat16)

        @pl.when(jnp.logical_not(has_before))
        def _():
            rb[t, c] = acc.astype(jnp.bfloat16)

        chain(t, c, slot, to).start()

    def down_slot(t):
        return jnp.where(t == i - 1, n_inter, t)

    def sums(s):
        up = n_inter - 1 - s

        each(s, ready)

        @pl.loop(0, chunks)
        def _(c):
            @pl.when(up > i)
            def _():
                hop(up, c, i > 0, up, i + 1)

            @pl.when(s < i)
            def _():
                hop(s, c, i < n_inter - 1, down_slot(s), i - 1)

    last = n_inter - 1

    @pl.loop(0, n_inter + 1)
    def _(s):
        @pl.when(s < last)
        def _():
            each(s, own)

        @pl.when(s == last)
        def _():
            own(i)

        @pl.when((s >= 1) & (s <= last))
        def _():
            each(s - 1, cross)

        @pl.when(s == last + 1)
        def _():
            cross(i)

        @pl.when(s >= 2)
        def _():
            sums(s - 2)

    ready(i)

    def total_of(c):
        acc = product(i, c)
        zero = jnp.zeros_like(acc)

        @pl.when(i > 0)
        def _():
            landed(i, c)

        @pl.when(i < n_inter - 1)
        def _():
            landed(n_inter, c)

        acc = acc + jnp.where(i > 0, rb[i, c].astype(jnp.float32), zero)
        return acc + jnp.where(i < n_inter - 1, rb[n_inter, c].astype(jnp.float32), zero)

    def rot(u):
        return u * cosb[...] + pltpu.roll(u, HD // 2, 1) * sinb[...]

    @pl.when(i == 0)
    def _():
        rb[0] = jnp.zeros(rb.shape[1:], rb.dtype)

    @pl.when(i == n_inter - 1)
    def _():
        rb[n_inter] = jnp.zeros(rb.shape[1:], rb.dtype)

    here_kv = width // HD
    per = n_intra // KV
    acc = total_of(0) + bkv[...].astype(jnp.float32)[None, :]
    for b in range(here_kv):
        gb = j * here_kv + b
        u = acc[:, b * HD:(b + 1) * HD]
        kvs[b] = jnp.where(gb < KV, rot(u), u).astype(jnp.bfloat16)

    def kv_copies(b, r):
        gb = j * here_kv + b
        dest = lax.rem(gb, KV) * per + r
        kind = gb // KV
        return dest, kind, remote(kvs.at[b], kvb.at[kind], kvsend.at[b * per + r],
                                  kvrecv.at[kind], i, dest)

    for b in range(here_kv):
        for r in range(per):
            dest, kind, cp = kv_copies(b, r)

            @pl.when(dest == j)
            def _():
                pltpu.make_async_copy(kvs.at[b], kvb.at[kind], kvrecv.at[kind]).start()

            @pl.when(dest != j)
            def _():
                cp.start()

    for kind in range(2):
        pltpu.make_async_copy(kvb.at[kind], kvb.at[kind], kvrecv.at[kind]).wait()

    for c in range(1, chunks):
        base = (c - 1) * width
        acc = total_of(c) + bq[base:base + width].astype(jnp.float32)[None, :]
        for h in range(width // HD):
            qh = rot(acc[:, h * HD:(h + 1) * HD]).astype(jnp.bfloat16)
            for b in range(batches):
                lo = b * block
                sc = lax.dot_general(qh[lo:lo + block, :], kvb[0, lo:lo + block, :],
                                     (((1,), (1,)), ((), ())),
                                     preferred_element_type=jnp.float32)
                sc = sc * HD ** (-0.5) + maskb[b]
                peak = jnp.max(sc, axis=-1, keepdims=True)
                expo = jnp.exp(sc - peak)
                wts = (expo / jnp.sum(expo, axis=-1, keepdims=True)).astype(jnp.bfloat16)
                ctx = jnp.dot(wts, kvb[1, lo:lo + block, :], preferred_element_type=jnp.float32)
                out[lo:lo + block, base + h * HD:base + (h + 1) * HD] = ctx.astype(jnp.bfloat16)

    for gg in range(layers_each):
        for p in range(n_intra):
            here, straight, keep, direct, detour = spread(gg, p)

            @pl.when(straight)
            def _():
                direct.wait_send()

            @pl.when(jnp.logical_not(here | straight))
            def _():
                detour.wait_send()

    @pl.loop(0, n_inter)
    def _(t):
        for cp in own_copies(t) + cross_copies(t):
            cp.wait_send()

        @pl.when(t != i)
        def _():
            @pl.when(detoured(t))
            def _():
                along(t).wait_send()

            @pl.loop(0, chunks)
            def _(c):
                chain(t, c, t, i).wait_send()

    for b in range(here_kv):
        for r in range(per):
            dest, kind, cp = kv_copies(b, r)

            @pl.when(dest != j)
            def _():
                cp.wait_send()


def local(n_inter, n_intra, hidden, w_query, w_keyval, b_query, b_keyval, segments):
    batches, block, feats = hidden.shape
    rows = batches * block
    depth, cols = w_query.shape
    width = w_keyval.shape[1]
    chunks = 1 + cols // width
    chips = n_intra // CORES
    vmem = pl.BlockSpec(memory_space=pltpu.VMEM)
    hbm = pl.BlockSpec(memory_space=pl.ANY)
    dma = pltpu.SemaphoreType.DMA
    here_kv = width // HD
    per = n_intra // KV
    result = pl.pallas_call(
        functools.partial(kernel, n_inter, n_intra),
        out_shape=jax.ShapeDtypeStruct((rows, cols), jnp.bfloat16),
        in_specs=[hbm, hbm, hbm, vmem, vmem, vmem],
        out_specs=vmem,
        scratch_shapes=[
            pltpu.VMEM((n_inter, rows, depth), jnp.bfloat16),
            pltpu.VMEM((n_inter, rows // n_intra, depth), jnp.bfloat16),
            pltpu.VMEM((chunks, depth, width), jnp.bfloat16),
            pltpu.VMEM((n_inter + 1, chunks, rows, width), jnp.bfloat16),
            pltpu.VMEM((rows, HD), jnp.float32),
            pltpu.VMEM((rows, HD), jnp.float32),
            pltpu.VMEM((batches, block, block), jnp.float32),
            pltpu.VMEM((here_kv, rows, HD), jnp.bfloat16),
            pltpu.VMEM((2, rows, HD), jnp.bfloat16),
            dma((chunks,)),
            dma((n_intra * (n_inter // n_intra),)),
            dma((n_inter,)),
            dma((n_inter,)),
            dma((n_inter,)),
            dma((n_inter, chips)),
            dma((n_inter, max(chips - 1, 1))),
            dma((n_inter, n_intra)),
            dma((n_inter, chunks)),
            dma((n_inter + 1, chunks)),
            dma((here_kv * per,)),
            dma((2,)),
        ],
        compiler_params=pltpu.CompilerParams(
            collective_id=0, has_side_effects=True, vmem_limit_bytes=52 * 2**20),
        name="project_attend",
    )(hidden.reshape(rows, feats), w_query, w_keyval, b_query, b_keyval, segments)
    return result.reshape(batches, block, cols)


def solution(mesh):
    in_specs = (
        P("grp", "inter", "intra"),
        P("inter", "intra"),
        P("inter", "intra"),
        P("intra"),
        P("intra"),
        P("grp", "inter", None),
    )
    out_specs = P("grp", "inter", "intra")
    body = functools.partial(local, mesh.shape["inter"], mesh.shape["intra"])
    return jax.shard_map(body, mesh=mesh, in_specs=in_specs, out_specs=out_specs, check_vma=False)
```

```python
import functools
import math

import jax
import jax.numpy as jnp
from jax import lax
from jax.experimental import pallas as pl
from jax.experimental.pallas import tpu as pltpu
from jax.sharding import PartitionSpec as P

QH = 32
KV = 4
HD = 128
CORES = 2
FALL = -2.0 * math.log(1000000.0) / HD
MESH = pl.DeviceIdType.MESH


def kernel(n_inter, n_intra, hid, wq, wkv, bq, bkv, seg, out,
           xg, stage, wbuf, rb, cosb, sinb, maskb, kvs, kvb,
           wsem, hsend, srecv, zsend, hrecv, fsend, xsend, frecv, csend, crecv, kvsend, kvrecv):
    batches, _, block = seg.shape
    rows = batches * block
    depth = wkv.shape[0]
    width = wkv.shape[1]
    chunks = wbuf.shape[0]
    piece = rows // n_intra
    layers_each = n_inter // n_intra
    chips = n_intra // CORES
    i = lax.axis_index("inter")
    j = lax.axis_index("intra")
    xc = j // CORES
    core = lax.rem(j, CORES)
    sibling = xc * CORES + (CORES - 1 - core)
    total = n_inter * n_intra
    me = i * n_intra + j

    wcopies = [pltpu.make_async_copy(wkv, wbuf.at[0], wsem.at[0])]
    for c in range(chunks - 1):
        wcopies.append(pltpu.make_async_copy(
            wq.at[:, pl.ds(c * width, width)], wbuf.at[c + 1], wsem.at[c + 1]))
    for cp in wcopies:
        cp.start()

    barrier = pltpu.get_barrier_semaphore()

    @pl.loop(1, total)
    def _(k):
        other = lax.rem(me + k, total)
        pl.semaphore_signal(
            barrier, inc=1,
            device_id={"inter": other // n_intra, "intra": lax.rem(other, n_intra)},
            device_id_type=MESH)

    pl.semaphore_wait(barrier, total - 1)

    def remote(src, dst, ssem, rsem, ii, jj):
        return pltpu.make_async_remote_copy(
            src_ref=src, dst_ref=dst, send_sem=ssem, recv_sem=rsem,
            device_id={"inter": ii, "intra": jj}, device_id_type=MESH)

    def spread(gg, p):
        layer = j * layers_each + gg
        src = hid.at[pl.ds(p * piece, piece), pl.ds(gg * depth, depth)]
        final = xg.at[i, pl.ds(p * piece, piece), :]
        sem = hsend.at[gg * n_intra + p]
        direct = remote(src, final, sem, hrecv.at[i], layer, p)
        detour = remote(src, stage.at[layer], sem, srecv.at[layer], i, p)
        keep = pltpu.make_async_copy(src, final, hrecv.at[i])
        here = (layer == i) & (p == j)
        straight = jnp.logical_not(here) & ((layer == i) | (p // CORES == xc))
        return here, straight, keep, direct, detour

    def layer_of(gg):
        return j * layers_each + gg

    for gg in range(layers_each):
        for p in range(n_intra):
            here, straight, keep, direct, detour = spread(gg, p)

            @pl.when(straight & (layer_of(gg) != i))
            def _():
                direct.start()

            @pl.when(jnp.logical_not(here | straight))
            def _():
                detour.start()

    def part(t, p):
        return xg.at[t, pl.ds(pl.multiple_of(p * piece, piece), piece), :]

    def along(t):
        return remote(stage.at[t], part(i, j), zsend.at[t], hrecv.at[i], t, j)

    def detoured(t):
        return (t // layers_each) // CORES != xc

    def each(s, fn):
        up = n_inter - 1 - s

        @pl.when((s >= 0) & (up > i))
        def _():
            fn(up)

        @pl.when((s >= 0) & (s < i))
        def _():
            fn(s)

    def onward(t):
        @pl.when(detoured(t))
        def _():
            pltpu.make_async_copy(stage.at[t], stage.at[t], srecv.at[t]).wait()
            along(t).start()

    @pl.loop(0, n_inter - 1)
    def _(s):
        each(s, onward)

    for gg in range(layers_each):
        for p in range(n_intra):
            here, straight, keep, direct, detour = spread(gg, p)

            @pl.when(here)
            def _():
                keep.start()

            @pl.when(straight & (layer_of(gg) == i))
            def _():
                direct.start()

    lane = lax.broadcasted_iota(jnp.int32, (1, HD), 1)
    fr = jnp.exp(lax.rem(lane, HD // 2).astype(jnp.float32) * FALL)
    r_i = lax.broadcasted_iota(jnp.int32, (block, block), 0)
    c_i = lax.broadcasted_iota(jnp.int32, (block, block), 1)
    place = lax.broadcasted_iota(jnp.int32, (block, 1), 0).astype(jnp.float32)

    def tables():
        for b in range(batches):
            segr = seg[b].astype(jnp.float32)
            segm = jnp.broadcast_to(segr, (block, block))
            segc = jnp.sum(jnp.where(r_i == c_i, segm, 0.0), axis=1, keepdims=True)
            below = jnp.sum(jnp.where(segm < segc, 1.0, 0.0), axis=1, keepdims=True)
            plen = jnp.sum(jnp.where(segm == 0.0, 1.0, 0.0), axis=1, keepdims=True)
            pos = place - below + jnp.where(segc > 0.0, plen, 0.0)
            angles = pos * fr
            cosb[b * block:(b + 1) * block, :] = jnp.cos(angles)
            sine = jnp.sin(angles)
            sinb[b * block:(b + 1) * block, :] = jnp.where(lane < HD // 2, -sine, sine)
            allowed = (c_i <= r_i) & ((segm == 0.0) | (segm == segc))
            maskb[b] = jnp.where(allowed, 0.0, -1e30)

    def own_copies(t):
        res = []
        for k in range(1, chips):
            ox = lax.rem(xc + k, chips)
            res.append(remote(part(t, j), part(t, j), fsend.at[t, k], frecv.at[t, j],
                              i, ox * CORES + core))
        res.append(remote(part(t, j), part(t, j), fsend.at[t, 0], frecv.at[t, j], i, sibling))
        return res

    def cross_copies(t):
        res = []
        for k in range(1, chips):
            p = lax.rem(xc + k, chips) * CORES + core
            res.append(remote(part(t, p), part(t, p), xsend.at[t, k - 1], frecv.at[t, p],
                              i, sibling))
        return res

    def arrived(t, p):
        pltpu.make_async_copy(part(t, p), part(t, p), frecv.at[t, p]).wait()

    def own(t):
        pltpu.make_async_copy(part(t, j), part(t, j), hrecv.at[t]).wait()
        for cp in own_copies(t):
            cp.start()

    def cross(t):
        for q in range(1, chips):
            arrived(t, lax.rem(xc + q, chips) * CORES + core)
        for cp in cross_copies(t):
            cp.start()

    tables()

    for cp in wcopies:
        cp.wait()

    def ready(t):
        for q in range(chips):
            arrived(t, q * CORES + (CORES - 1 - core))

    def product(t, c):
        return jnp.dot(xg[t], wbuf[c], preferred_element_type=jnp.float32)

    def chain(t, c, slot, to):
        return remote(rb.at[t, c], rb.at[slot, c], csend.at[t, c], crecv.at[slot, c], to, j)

    def landed(slot, c):
        pltpu.make_async_copy(rb.at[slot, c], rb.at[slot, c], crecv.at[slot, c]).wait()

    def hop(t, c, has_before, slot, to):
        acc = product(t, c)

        @pl.when(has_before)
        def _():
            landed(t, c)
            rb[t, c] = (rb[t, c].astype(jnp.float32) + acc).astype(jnp.bfloat16)

        @pl.when(jnp.logical_not(has_before))
        def _():
            rb[t, c] = acc.astype(jnp.bfloat16)

        chain(t, c, slot, to).start()

    def down_slot(t):
        return jnp.where(t == i - 1, n_inter, t)

    def sums(s):
        up = n_inter - 1 - s

        each(s, ready)

        @pl.loop(0, chunks)
        def _(c):
            @pl.when(up > i)
            def _():
                hop(up, c, i > 0, up, i + 1)

            @pl.when(s < i)
            def _():
                hop(s, c, i < n_inter - 1, down_slot(s), i - 1)

    last = n_inter - 1

    @pl.loop(0, n_inter + 1)
    def _(s):
        @pl.when(s < last)
        def _():
            each(s, own)

        @pl.when(s == last)
        def _():
            own(i)

        @pl.when((s >= 1) & (s <= last))
        def _():
            each(s - 1, cross)

        @pl.when(s == last + 1)
        def _():
            cross(i)

        @pl.when(s >= 2)
        def _():
            sums(s - 2)

    ready(i)

    def total_of(c):
        acc = product(i, c)
        zero = jnp.zeros_like(acc)

        @pl.when(i > 0)
        def _():
            landed(i, c)

        @pl.when(i < n_inter - 1)
        def _():
            landed(n_inter, c)

        acc = acc + jnp.where(i > 0, rb[i, c].astype(jnp.float32), zero)
        return acc + jnp.where(i < n_inter - 1, rb[n_inter, c].astype(jnp.float32), zero)

    def rot(u):
        return u * cosb[...] + pltpu.roll(u, HD // 2, 1) * sinb[...]

    @pl.when(i == 0)
    def _():
        rb[0] = jnp.zeros(rb.shape[1:], rb.dtype)

    @pl.when(i == n_inter - 1)
    def _():
        rb[n_inter] = jnp.zeros(rb.shape[1:], rb.dtype)

    here_kv = width // HD
    per = n_intra // KV
    acc = total_of(0) + bkv[...].astype(jnp.float32)[None, :]
    for b in range(here_kv):
        gb = j * here_kv + b
        u = acc[:, b * HD:(b + 1) * HD]
        kvs[b] = jnp.where(gb < KV, rot(u), u).astype(jnp.bfloat16)

    def kv_copies(b, r):
        gb = j * here_kv + b
        dest = lax.rem(gb, KV) * per + r
        kind = gb // KV
        return dest, kind, remote(kvs.at[b], kvb.at[kind], kvsend.at[b * per + r],
                                  kvrecv.at[kind], i, dest)

    for b in range(here_kv):
        for r in range(per):
            dest, kind, cp = kv_copies(b, r)

            @pl.when(dest == j)
            def _():
                pltpu.make_async_copy(kvs.at[b], kvb.at[kind], kvrecv.at[kind]).start()

            @pl.when(dest != j)
            def _():
                cp.start()

    for kind in range(2):
        pltpu.make_async_copy(kvb.at[kind], kvb.at[kind], kvrecv.at[kind]).wait()

    for c in range(1, chunks):
        base = (c - 1) * width
        acc = total_of(c) + bq[base:base + width].astype(jnp.float32)[None, :]
        for h in range(width // HD):
            qh = rot(acc[:, h * HD:(h + 1) * HD]).astype(jnp.bfloat16)
            for b in range(batches):
                lo = b * block
                sc = lax.dot_general(qh[lo:lo + block, :], kvb[0, lo:lo + block, :],
                                     (((1,), (1,)), ((), ())),
                                     preferred_element_type=jnp.float32)
                sc = sc * HD ** (-0.5) + maskb[b]
                peak = jnp.max(sc, axis=-1, keepdims=True)
                expo = jnp.exp(sc - peak)
                wts = (expo / jnp.sum(expo, axis=-1, keepdims=True)).astype(jnp.bfloat16)
                ctx = jnp.dot(wts, kvb[1, lo:lo + block, :], preferred_element_type=jnp.float32)
                out[lo:lo + block, base + h * HD:base + (h + 1) * HD] = ctx.astype(jnp.bfloat16)

    for gg in range(layers_each):
        for p in range(n_intra):
            here, straight, keep, direct, detour = spread(gg, p)

            @pl.when(straight)
            def _():
                direct.wait_send()

            @pl.when(jnp.logical_not(here | straight))
            def _():
                detour.wait_send()

    @pl.loop(0, n_inter)
    def _(t):
        for cp in own_copies(t) + cross_copies(t):
            cp.wait_send()

        @pl.when(t != i)
        def _():
            @pl.when(detoured(t))
            def _():
                along(t).wait_send()

            @pl.loop(0, chunks)
            def _(c):
                chain(t, c, t, i).wait_send()

    for b in range(here_kv):
        for r in range(per):
            dest, kind, cp = kv_copies(b, r)

            @pl.when(dest != j)
            def _():
                cp.wait_send()


def local(n_inter, n_intra, hidden, w_query, w_keyval, b_query, b_keyval, segments):
    batches, block, feats = hidden.shape
    rows = batches * block
    depth, cols = w_query.shape
    width = w_keyval.shape[1]
    chunks = 1 + cols // width
    chips = n_intra // CORES
    vmem = pl.BlockSpec(memory_space=pltpu.VMEM)
    hbm = pl.BlockSpec(memory_space=pl.ANY)
    dma = pltpu.SemaphoreType.DMA
    here_kv = width // HD
    per = n_intra // KV
    result = pl.pallas_call(
        functools.partial(kernel, n_inter, n_intra),
        out_shape=jax.ShapeDtypeStruct((rows, cols), jnp.bfloat16),
        in_specs=[hbm, hbm, hbm, vmem, vmem, vmem],
        out_specs=vmem,
        scratch_shapes=[
            pltpu.VMEM((n_inter, rows, depth), jnp.bfloat16),
            pltpu.VMEM((n_inter, rows // n_intra, depth), jnp.bfloat16),
            pltpu.VMEM((chunks, depth, width), jnp.bfloat16),
            pltpu.VMEM((n_inter + 1, chunks, rows, width), jnp.bfloat16),
            pltpu.VMEM((rows, HD), jnp.float32),
            pltpu.VMEM((rows, HD), jnp.float32),
            pltpu.VMEM((batches, block, block), jnp.float32),
            pltpu.VMEM((here_kv, rows, HD), jnp.bfloat16),
            pltpu.VMEM((2, rows, HD), jnp.bfloat16),
            dma((chunks,)),
            dma((n_intra * (n_inter // n_intra),)),
            dma((n_inter,)),
            dma((n_inter,)),
            dma((n_inter,)),
            dma((n_inter, chips)),
            dma((n_inter, max(chips - 1, 1))),
            dma((n_inter, n_intra)),
            dma((n_inter, chunks)),
            dma((n_inter + 1, chunks)),
            dma((here_kv * per,)),
            dma((2,)),
        ],
        compiler_params=pltpu.CompilerParams(
            collective_id=0, has_side_effects=True, vmem_limit_bytes=52 * 2**20),
        name="project_attend",
    )(hidden.reshape(rows, feats), w_query, w_keyval, b_query, b_keyval, segments)
    return result.reshape(batches, block, cols)


def solution(mesh):
    in_specs = (
        P("grp", "inter", "intra"),
        P("inter", "intra"),
        P("inter", "intra"),
        P("intra"),
        P("intra"),
        P("grp", "inter", None),
    )
    out_specs = P("grp", "inter", "intra")
    body = functools.partial(local, mesh.shape["inter"], mesh.shape["intra"])
    return jax.shard_map(body, mesh=mesh, in_specs=in_specs, out_specs=out_specs, check_vma=False)
```
